128 devices in a mesh: dp: 8 (over x, core), vocab: 16 (over y, z).
Axes of the slice: x: 4, y: 4, z: 4, core: 2. Of those that a mesh axis runs over, the one named last changes fastest.
Arguments:
- hidden_rows: bfloat16 [5120, 2048], P(('dp', 'vocab')), parts along dimension 0, may hold values from -10 to 10
- head_weight: bfloat16 [2048, 77824], P(None, 'vocab'), may hold values from -0.15 to 1
Outputs:
- token_probs: bfloat16 [5120, 77824], P('dp', 'vocab'), parts along dimension 0
The draws below stay inside these ranges and needn't reach their ends.
There are 8 independent parts, one for each index of `dp`. The reference program is written for one: setup_inputs(seed, part) draws one part's arguments, and reference() takes and returns one part's arrays. A program takes and returns all parts, laid end to end along the dimension named above; an argument that names none is the same for every part. Nothing has to cross between parts.
All inputs are finite; a program needn't handle non-finite values.
Results may differ from the reference program's by a relative error of at most 0.012.
Values may be sent and summed in bfloat16 or wider, within the bound.
A program may use at most 128 MiB of HBM per device.

```python
import math
import jax
import jax.numpy as jnp

D = 2048
VOC_DEV = 4864
ROWS = 640
VOCAB = 77824


def draw_hidden_rows(key, part):
    key = jax.random.fold_in(key, 1)
    subkeys = jax.random.split(key, 7)
    shards = VOCAB // VOC_DEV
    places = 4 * shards
    values = jnp.clip(jax.random.normal(subkeys[0], (ROWS, D), jnp.float32), -6.0, 6.0)
    log_scale = jax.random.uniform(subkeys[1], (ROWS, 1), jnp.float32, math.log(0.5), math.log(1.2))
    spread = jnp.exp(log_scale)
    margin = jax.random.uniform(subkeys[2], (ROWS, 1), jnp.float32, 0.2, 2.5)
    summit = 4.4 * spread + margin
    leader = jax.random.randint(subkeys[3], (ROWS, 1), 0, shards)
    first_pick = jax.random.randint(subkeys[4], (ROWS, 1), 1, shards)
    second = 1 + (first_pick - 1 + jax.random.randint(subkeys[5], (ROWS, 1), 1, shards - 1)) % (shards - 1)
    position = jnp.arange(places)
    holder = position // 4
    member = position % 4
    relative = (holder[None, :] - leader) % shards
    active = (relative == first_pick) | (relative == second)
    fraction = jax.random.uniform(subkeys[6], (ROWS, places), jnp.float32)
    nearby = jnp.where(member == 0, 1.0 + 1.4 * fraction, jnp.where(member == 1, 2.996 - 0.2 * fraction, jnp.where(member == 2, 2.996 + 0.2 * fraction, 2.7 + 0.6 * fraction)))
    offset = jnp.where(active, nearby, 4.0 + 5.0 * fraction)
    offset = jnp.where((relative == 0) & (member == 0), 0.0, offset)
    values = jnp.concatenate([summit - offset, spread * values[:, places:]], axis=1)
    return values.astype(jnp.bfloat16)


def draw_head_weight(key, part):
    key = jax.random.fold_in(key, 2)
    shards = VOCAB // VOC_DEV
    cluster_size = max(VOC_DEV // 38, 2)
    random_part = jnp.clip(jax.random.normal(key, (D, VOCAB), jnp.float32), -6.0, 6.0) / math.sqrt(D)
    column = jnp.arange(VOCAB)
    within = column % VOC_DEV
    clustered = within < 1 + 3 * cluster_size
    member = jnp.where(within == 0, 0, (within - 1) // cluster_size + 1)
    target = column // VOC_DEV * 4 + member
    row_index = jnp.arange(D)[:, None]
    factor = jnp.where(clustered[None, :], 0.02, jnp.where(row_index < 4 * shards, 0.02, 1.0))
    boosts = jnp.where((row_index == target[None, :]) & clustered[None, :], 1.0, 0.0)
    values = jnp.clip(random_part * factor + boosts, -0.149, 1.0)
    return values.astype(jnp.bfloat16)


def setup_inputs(seed: int = 0, part: int = 0) -> dict:
    keys = jax.random.split(jax.random.key(seed), 3)
    part_keys = jax.random.split(jax.random.fold_in(keys[2], part), 3)
    hidden_rows = draw_hidden_rows(jax.random.fold_in(jax.random.fold_in(keys[2], part), 71), part)
    head_weight = draw_head_weight(jax.random.fold_in(keys[2], 71), part)
    return dict(hidden_rows=hidden_rows, head_weight=head_weight)


def reference(hidden_rows, head_weight):
    logits = jnp.dot(hidden_rows, head_weight, preferred_element_type=jnp.float32)
    peak = jnp.max(logits, axis=1)
    ratio = jnp.exp(logits - peak[:, None])
    kept = ratio * jnp.clip((ratio - 0.05) / 0.05, 0.0, 1.0)
    mass = jnp.sum(kept, axis=1)
    return (kept / mass[:, None]).astype(jnp.bfloat16)
```

```python
import jax
import jax.numpy as jnp
from jax import lax
from jax.experimental import pallas as pl
from jax.experimental.pallas import tpu as pltpu
from jax.sharding import PartitionSpec as P

MESH = pl.DeviceIdType.MESH
F32 = jnp.float32
BLOCK = 40
HALF = 1024
GROUPS = (
    ((0, 0), (3, 0), (1, 0), (0, 1)),
    ((0, 3), (2, 0), (3, 1), (3, 3)),
    ((1, 1), (1, 3), (2, 1), (2, 3)),
    ((0, 2), (3, 2), (1, 2), (2, 2)),
)
ARRIVALS = (
    (3, 0, "w"), (1, 0, "w"), (2, 0, 0), (2, 0, 1),
    (0, 3, "w"), (0, 1, "w"), (3, 3, "w"), (3, 1, "w"), (1, 3, "w"), (1, 1, "w"), (2, 3, "w"), (2, 1, "w"),
    (0, 2, "w"), (3, 2, "w"), (1, 2, 0), (1, 2, 1), (2, 2, 0), (2, 2, 1),
)


def to_row(tile):
    return jnp.transpose(tile)


def to_column(row):
    return jnp.transpose(jnp.broadcast_to(row, (128, 128)))


def kernel(x_hbm, w_hbm, kept, scale, w, xb, xs, lane, peak_col, row_send, row_recv,
           w_sem, own_sem, send_sem, recv_sem, row_send_sem, row_recv_sem):
    core = lax.rem(lax.axis_index("dp"), 2)
    me = lax.axis_index("vocab")
    y, z = me // 4, lax.rem(me, 4)
    a, b = z + core * (y - z), y + core * (z - y)
    stride_a, stride_b = 1 + 3 * core, 4 - 3 * core

    def block(da, db):
        return lax.rem(a + da, 4) * stride_a + lax.rem(b + db, 4) * stride_b

    def rows_of(da, db):
        return pl.ds(pl.multiple_of(block(da, db) * BLOCK, 8), BLOCK)

    w_copy = pltpu.make_async_copy(w_hbm, w, w_sem)
    w_copy.start()
    own_copy = pltpu.make_async_copy(x_hbm, xb.at[me], own_sem)
    own_copy.start()

    barrier = pltpu.get_barrier_semaphore()
    neighbours = (block(1, 0), block(3, 0), block(0, 1), block(0, 3))
    for peer in neighbours:
        pl.semaphore_signal(barrier, inc=1, device_id={"vocab": peer}, device_id_type=MESH)
    pl.semaphore_wait(barrier, 4)

    started = []

    def part(ref, half):
        return ref if half == "w" else ref.at[:, pl.ds(half * HALF, HALF)]

    def send(da, db, half, to):
        ta, tb = to
        slot = ARRIVALS.index(((da - ta) % 4, (db - tb) % 4, half))
        here = x_hbm if (da, db) == (0, 0) else xb.at[block(da, db)]
        copy = pltpu.make_async_remote_copy(
            src_ref=part(here, half),
            dst_ref=part(xb.at[block(da, db)], half),
            send_sem=send_sem.at[slot],
            recv_sem=recv_sem.at[slot],
            device_id={"vocab": block(ta, tb)},
            device_id_type=MESH,
        )
        copy.start()
        started.append(copy)

    def arrive(da, db, half):
        slot = ARRIVALS.index((da, db, half))
        ref = part(xb.at[block(da, db)], half)
        pltpu.make_async_copy(ref, ref, recv_sem.at[slot]).wait()

    A_UP, A_DOWN, B_UP, B_DOWN = (1, 0), (3, 0), (0, 1), (0, 3)

    def multiply(group, columns):
        at = [rows_of(*g) for g in group]
        first = columns[0] == 0
        best = None if first else [lane[r, :] for r in at]
        for c in range(columns[0], columns[1], 256):
            out = jnp.dot(xs[...], w[:, c:c + 256], preferred_element_type=F32)
            for i, r in enumerate(at):
                piece = out[i * BLOCK:(i + 1) * BLOCK]
                kept[r, c:c + 256] = piece
                top = jnp.maximum(piece[:, :128], piece[:, 128:])
                if best is None or len(best) <= i:
                    best = (best or []) + [top]
                else:
                    best[i] = jnp.maximum(best[i], top)
        for i, r in enumerate(at):
            lane[r, :] = best[i]

    def gather_group(group):
        xs[...] = jnp.concatenate([xb[block(*g)] for g in group], axis=0)

    send(0, 0, "w", A_UP)
    send(0, 0, "w", A_DOWN)
    send(0, 0, "w", B_UP)
    send(0, 0, "w", B_DOWN)
    own_copy.wait()
    arrive(3, 0, "w")
    send(3, 0, 0, A_UP)
    send(3, 0, "w", B_UP)
    send(3, 0, "w", B_DOWN)
    arrive(1, 0, "w")
    send(1, 0, 1, A_DOWN)
    send(1, 0, "w", B_UP)
    send(1, 0, "w", B_DOWN)
    arrive(0, 3, "w")
    send(0, 3, "w", B_UP)
    arrive(0, 1, "w")
    w_copy.wait()
    gather_group(GROUPS[0])
    multiply(GROUPS[0], (0, 2304))
    arrive(2, 0, 0)
    arrive(2, 0, 1)
    send(2, 0, "w", B_UP)
    send(2, 0, "w", B_DOWN)
    multiply(GROUPS[0], (2304, 4864))
    arrive(3, 3, "w")
    arrive(3, 1, "w")
    send(3, 1, "w", B_DOWN)
    gather_group(GROUPS[1])
    multiply(GROUPS[1], (0, 2304))
    arrive(1, 3, "w")
    send(1, 3, 0, B_UP)
    arrive(1, 1, "w")
    send(1, 1, 1, B_DOWN)
    multiply(GROUPS[1], (2304, 4864))
    arrive(2, 3, "w")
    send(2, 3, 0, B_UP)
    arrive(2, 1, "w")
    send(2, 1, 1, B_DOWN)
    gather_group(GROUPS[2])
    multiply(GROUPS[2], (0, 4864))
    for last in ARRIVALS[12:]:
        arrive(*last)
    gather_group(GROUPS[3])
    multiply(GROUPS[3], (0, 4864))

    def exchange(step):
        for i in range(1, 16):
            copy = pltpu.make_async_remote_copy(
                src_ref=row_send.at[step],
                dst_ref=row_recv.at[step, 15 - i],
                send_sem=row_send_sem.at[step],
                recv_sem=row_recv_sem.at[step],
                device_id={"vocab": lax.rem(me + i, 16)},
                device_id_type=MESH,
            )
            copy.start()

    def exchanged(step):
        pltpu.make_async_copy(row_recv.at[step], row_recv.at[step], row_recv_sem.at[step]).wait()

    tiles = [slice(i * 128, (i + 1) * 128) for i in range(5)]
    for t in tiles:
        row_send[0, :, t] = jnp.max(to_row(lane[t, :]), axis=0, keepdims=True)
    exchange(0)
    for t in tiles:
        peak_col[t, :] = to_column(row_send[0, :, t])

    @pl.loop(0, 40)
    def _(i):
        r = pl.ds(pl.multiple_of(i * 16, 16), 16)
        top = peak_col[r, :]
        for c in range(0, 4864, 128):
            kept[r, c:c + 128] = jnp.exp(kept[r, c:c + 128] - top)

    exchanged(0)
    local = row_send[0]
    peak = jnp.maximum(local, jnp.max(row_recv[0], axis=0))
    shrink = jnp.exp(local - peak)
    for t in tiles:
        peak_col[t, :] = to_column(shrink[:, t] * 20.0)

    @pl.loop(0, 40)
    def _(i):
        r = pl.ds(pl.multiple_of(i * 16, 16), 16)
        factor = peak_col[r, :]
        total = jnp.zeros((16, 128), F32)
        for c in range(0, 4864, 128):
            ratio = kept[r, c:c + 128]
            value = ratio * jnp.clip(ratio * factor - 1.0, 0.0, 1.0)
            kept[r, c:c + 128] = value
            total = total + value
        lane[r, :] = total

    for t in tiles:
        row_send[1, :, t] = jnp.sum(to_row(lane[t, :]), axis=0, keepdims=True) * shrink[:, t]
    exchange(1)
    exchanged(1)
    mass = row_send[1] + jnp.sum(row_recv[1], axis=0)
    final = shrink / mass
    for t in tiles:
        scale[t, :] = to_column(final[:, t])

    for copy in started:
        copy.wait_send()
    for step in range(2):
        pltpu.make_async_copy(row_recv.at[step], row_recv.at[step], row_send_sem.at[step]).wait()


def finish(kept, scale, out, stage, sem):
    copies = []
    for i in range(10):
        @pl.loop(0, 4)
        def _(j):
            r = pl.ds(pl.multiple_of(i * 64 + j * 16, 16), 16)
            factor = scale[r, :]
            for c in range(0, 4864, 128):
                stage[r, c:c + 128] = (kept[r, c:c + 128] * factor).astype(jnp.bfloat16)
        rows = pl.ds(i * 64, 64)
        copy = pltpu.make_async_copy(stage.at[rows, :], out.at[rows, :], sem.at[i])
        copy.start()
        copies.append(copy)
    for copy in copies:
        copy.wait()


def body(hidden_rows, head_weight):
    kept, scale = pl.pallas_call(
        kernel,
        out_shape=(pltpu.VMEM((640, 4864), F32), pltpu.VMEM((640, 128), F32)),
        in_specs=[pl.BlockSpec(memory_space=pl.ANY)] * 2,
        out_specs=(pl.BlockSpec(memory_space=pltpu.VMEM),) * 2,
        scratch_shapes=[
            pltpu.VMEM((2048, 4864), jnp.bfloat16),
            pltpu.VMEM((16, BLOCK, 2048), jnp.bfloat16),
            pltpu.VMEM((4 * BLOCK, 2048), jnp.bfloat16),
            pltpu.VMEM((640, 128), F32),
            pltpu.VMEM((640, 128), F32),
            pltpu.VMEM((2, 1, 640), F32),
            pltpu.VMEM((2, 15, 1, 640), F32),
            pltpu.SemaphoreType.DMA,
            pltpu.SemaphoreType.DMA,
            pltpu.SemaphoreType.DMA((18,)),
            pltpu.SemaphoreType.DMA((18,)),
            pltpu.SemaphoreType.DMA((2,)),
            pltpu.SemaphoreType.DMA((2,)),
        ],
        compiler_params=pltpu.CompilerParams(
            collective_id=0, has_side_effects=True, vmem_limit_bytes=32 * 2**20
        ),
        cost_estimate=pl.CostEstimate(flops=2 * 640 * 2048 * 4864, bytes_accessed=36 * 10**6, transcendentals=640 * 4864),
    )(hidden_rows, head_weight)
    kept = pltpu.with_memory_space_constraint(kept, pltpu.VMEM)
    scale = pltpu.with_memory_space_constraint(scale, pltpu.VMEM)
    return pl.pallas_call(
        finish,
        out_shape=jax.ShapeDtypeStruct((640, 4864), jnp.bfloat16),
        in_specs=[pl.BlockSpec(memory_space=pltpu.VMEM)] * 2,
        out_specs=pl.BlockSpec(memory_space=pl.ANY),
        scratch_shapes=[pltpu.VMEM((640, 4864), jnp.bfloat16), pltpu.SemaphoreType.DMA((10,))],
        compiler_params=pltpu.CompilerParams(vmem_limit_bytes=10 * 2**20),
        cost_estimate=pl.CostEstimate(flops=640 * 4864, bytes_accessed=19 * 10**6, transcendentals=0),
    )(kept, scale)


def solution(mesh):
    in_specs = (P(("dp", "vocab"), None), P(None, "vocab"))
    out_specs = P("dp", "vocab")
    return jax.shard_map(body, mesh=mesh, in_specs=in_specs, out_specs=out_specs, check_vma=False)
```

```python
import jax
import jax.numpy as jnp
from jax import lax
from jax.experimental import pallas as pl
from jax.experimental.pallas import tpu as pltpu
from jax.sharding import PartitionSpec as P

MESH = pl.DeviceIdType.MESH
F32 = jnp.float32
BLOCK = 40
HALF = 1024
GROUPS = (
    ((0, 0), (3, 0), (1, 0)),
    ((2, 0), (0, 3), (0, 1)),
    ((3, 3), (3, 1), (1, 3), (1, 1)),
    ((2, 3), (2, 1), (0, 2)),
    ((3, 2), (1, 2), (2, 2)),
)
ARRIVALS = tuple((da, db, half) for da in range(4) for db in range(4) for half in (0, 1) if (da, db) != (0, 0))
PEERS = tuple(sorted(
    ((da, db) for da in range(4) for db in range(4) if (da, db) != (0, 0)),
    key=lambda p: -(min(p[0], 4 - p[0]) + min(p[1], 4 - p[1])),
))


def to_row(tile):
    return jnp.transpose(tile)


def to_column(row):
    return jnp.transpose(jnp.broadcast_to(row, (128, 128)))


def kernel(x_hbm, w_hbm, kept, scale, w, xb, xs, lane, peak_col, row_send, row_recv,
           w_sem, own_sem, send_sem, recv_sem, row_send_sem, row_recv_sem):
    core = lax.rem(lax.axis_index("dp"), 2)
    me = lax.axis_index("vocab")
    y, z = me // 4, lax.rem(me, 4)
    a, b = z + core * (y - z), y + core * (z - y)
    stride_a, stride_b = 1 + 3 * core, 4 - 3 * core

    def block(da, db):
        return lax.rem(a + da, 4) * stride_a + lax.rem(b + db, 4) * stride_b

    def rows_of(da, db):
        return pl.ds(pl.multiple_of(block(da, db) * BLOCK, 8), BLOCK)

    w_copy = pltpu.make_async_copy(w_hbm, w, w_sem)
    w_copy.start()
    own_copy = pltpu.make_async_copy(x_hbm, xb.at[me], own_sem)
    own_copy.start()

    barrier = pltpu.get_barrier_semaphore()
    neighbours = (block(1, 0), block(3, 0), block(0, 1), block(0, 3))
    for peer in neighbours:
        pl.semaphore_signal(barrier, inc=1, device_id={"vocab": peer}, device_id_type=MESH)
    pl.semaphore_wait(barrier, 4)

    started = []

    def part(ref, half):
        return ref.at[:, pl.ds(half * HALF, HALF)]

    def send(da, db, half, *directions):
        for ta, tb in directions:
            slot = ARRIVALS.index(((da - ta) % 4, (db - tb) % 4, half))
            ref = part(xb.at[block(da, db)], half)
            copy = pltpu.make_async_remote_copy(
                src_ref=ref,
                dst_ref=ref,
                send_sem=send_sem.at[slot],
                recv_sem=recv_sem.at[slot],
                device_id={"vocab": block(ta, tb)},
                device_id_type=MESH,
            )
            copy.start()
            started.append(copy)

    def arrive(da, db, *halves):
        for half in halves:
            slot = ARRIVALS.index((da, db, half))
            ref = part(xb.at[block(da, db)], half)
            pltpu.make_async_copy(ref, ref, recv_sem.at[slot]).wait()

    A_UP, A_DOWN, B_UP, B_DOWN = (1, 0), (3, 0), (0, 1), (0, 3)

    def multiply(group, columns):
        at = [rows_of(*g) for g in group]
        first = columns[0] == 0
        best = None if first else [lane[r, :] for r in at]
        for c in range(columns[0], columns[1], 256):
            out = jnp.dot(xs[:len(group) * BLOCK, :], w[:, c:c + 256], preferred_element_type=F32)
            for i, r in enumerate(at):
                piece = out[i * BLOCK:(i + 1) * BLOCK]
                kept[r, c:c + 256] = piece
                top = jnp.maximum(piece[:, :128], piece[:, 128:])
                if best is None or len(best) <= i:
                    best = (best or []) + [top]
                else:
                    best[i] = jnp.maximum(best[i], top)
        for i, r in enumerate(at):
            lane[r, :] = best[i]

    def gather_group(group):
        xs[:len(group) * BLOCK, :] = jnp.concatenate([xb[block(*g)] for g in group], axis=0)

    own_copy.wait()
    send(0, 0, 0, A_UP)
    send(0, 0, 1, A_DOWN)
    send(0, 0, 1, A_UP)
    send(0, 0, 0, A_DOWN)
    send(0, 0, 0, B_UP)
    send(0, 0, 1, B_DOWN)
    send(0, 0, 1, B_UP)
    send(0, 0, 0, B_DOWN)
    arrive(3, 0, 0)
    send(3, 0, 0, A_UP)
    arrive(1, 0, 1)
    send(1, 0, 1, A_DOWN)
    send(3, 0, 0, B_UP, B_DOWN)
    send(1, 0, 1, B_UP, B_DOWN)
    arrive(3, 0, 1)
    send(3, 0, 1, B_UP, B_DOWN)
    arrive(1, 0, 0)
    send(1, 0, 0, B_UP, B_DOWN)
    arrive(0, 3, 0)
    send(0, 3, 0, B_UP)
    arrive(0, 1, 1)
    send(0, 1, 1, B_DOWN)
    w_copy.wait()
    gather_group(GROUPS[0])
    multiply(GROUPS[0], (0, 2304))
    arrive(2, 0, 0)
    send(2, 0, 0, B_UP, B_DOWN)
    arrive(2, 0, 1)
    send(2, 0, 1, B_UP, B_DOWN)
    multiply(GROUPS[0], (2304, 4864))
    arrive(0, 3, 1)
    arrive(0, 1, 0)
    gather_group(GROUPS[1])
    multiply(GROUPS[1], (0, 2304))
    arrive(3, 3, 0)
    send(3, 3, 0, B_UP)
    arrive(3, 1, 1)
    send(3, 1, 1, B_DOWN)
    multiply(GROUPS[1], (2304, 4864))
    arrive(1, 3, 0)
    send(1, 3, 0, B_UP)
    arrive(1, 1, 1)
    send(1, 1, 1, B_DOWN)
    arrive(3, 3, 1)
    arrive(3, 1, 0)
    arrive(1, 3, 1)
    arrive(1, 1, 0)
    gather_group(GROUPS[2])
    multiply(GROUPS[2], (0, 2304))
    arrive(2, 3, 0)
    send(2, 3, 0, B_UP)
    arrive(2, 1, 1)
    send(2, 1, 1, B_DOWN)
    multiply(GROUPS[2], (2304, 4864))
    arrive(2, 3, 1)
    arrive(2, 1, 0)
    arrive(0, 2, 0, 1)
    gather_group(GROUPS[3])
    multiply(GROUPS[3], (0, 4864))
    arrive(3, 2, 0, 1)
    arrive(1, 2, 0, 1)
    arrive(2, 2, 0, 1)
    gather_group(GROUPS[4])
    multiply(GROUPS[4], (0, 4864))

    def exchange(step):
        for i, peer in enumerate(PEERS):
            copy = pltpu.make_async_remote_copy(
                src_ref=row_send.at[step],
                dst_ref=row_recv.at[step, i],
                send_sem=row_send_sem.at[step],
                recv_sem=row_recv_sem.at[step],
                device_id={"vocab": block(*peer)},
                device_id_type=MESH,
            )
            copy.start()

    def exchanged(step):
        pltpu.make_async_copy(row_recv.at[step], row_recv.at[step], row_recv_sem.at[step]).wait()

    tiles = [slice(i * 128, (i + 1) * 128) for i in range(5)]
    for t in tiles:
        row_send[0, :, t] = jnp.max(to_row(lane[t, :]), axis=0, keepdims=True)
    exchange(0)
    for t in tiles:
        peak_col[t, :] = to_column(row_send[0, :, t])

    @pl.loop(0, 20)
    def _(i):
        r = pl.ds(pl.multiple_of(i * 32, 32), 32)
        top = peak_col[r, :]
        for c in range(0, 4864, 128):
            kept[r, c:c + 128] = jnp.exp(kept[r, c:c + 128] - top)

    exchanged(0)
    local = row_send[0]
    peak = jnp.maximum(local, jnp.max(row_recv[0], axis=0))
    shrink = jnp.exp(local - peak)
    for t in tiles:
        peak_col[t, :] = to_column(shrink[:, t] * 20.0)

    @pl.loop(0, 20)
    def _(i):
        r = pl.ds(pl.multiple_of(i * 32, 32), 32)
        factor = peak_col[r, :]
        total = jnp.zeros((32, 128), F32)
        for c in range(0, 4864, 128):
            ratio = kept[r, c:c + 128]
            value = ratio * jnp.clip(ratio * factor - 1.0, 0.0, 1.0)
            kept[r, c:c + 128] = value
            total = total + value
        lane[r, :] = total

    for t in tiles:
        row_send[1, :, t] = jnp.sum(to_row(lane[t, :]), axis=0, keepdims=True) * shrink[:, t]
    exchange(1)
    exchanged(1)
    mass = row_send[1] + jnp.sum(row_recv[1], axis=0)
    final = shrink / mass
    for t in tiles:
        scale[t, :] = to_column(final[:, t])

    for copy in started:
        copy.wait_send()
    for step in range(2):
        pltpu.make_async_copy(row_recv.at[step], row_recv.at[step], row_send_sem.at[step]).wait()


def finish(kept, scale, out, stage, sem):
    copies = []
    for i in range(20):
        @pl.loop(0, 2)
        def _(j):
            r = pl.ds(pl.multiple_of(i * 32 + j * 16, 16), 16)
            factor = scale[r, :]
            for c in range(0, 4864, 128):
                stage[r, c:c + 128] = (kept[r, c:c + 128] * factor).astype(jnp.bfloat16)
        rows = pl.ds(i * 32, 32)
        copy = pltpu.make_async_copy(stage.at[rows, :], out.at[rows, :], sem.at[i])
        copy.start()
        copies.append(copy)
    for copy in copies:
        copy.wait()


def body(hidden_rows, head_weight):
    hidden_rows = pltpu.with_memory_space_constraint(hidden_rows, pltpu.HBM)
    kept, scale = pl.pallas_call(
        kernel,
        out_shape=(pltpu.VMEM((640, 4864), F32), pltpu.VMEM((640, 128), F32)),
        in_specs=[pl.BlockSpec(memory_space=pltpu.HBM)] * 2,
        out_specs=(pl.BlockSpec(memory_space=pltpu.VMEM),) * 2,
        scratch_shapes=[
            pltpu.VMEM((2048, 4864), jnp.bfloat16),
            pltpu.VMEM((16, BLOCK, 2048), jnp.bfloat16),
            pltpu.VMEM((4 * BLOCK, 2048), jnp.bfloat16),
            pltpu.VMEM((640, 128), F32),
            pltpu.VMEM((640, 128), F32),
            pltpu.VMEM((2, 1, 640), F32),
            pltpu.VMEM((2, 15, 1, 640), F32),
            pltpu.SemaphoreType.DMA,
            pltpu.SemaphoreType.DMA,
            pltpu.SemaphoreType.DMA((30,)),
            pltpu.SemaphoreType.DMA((30,)),
            pltpu.SemaphoreType.DMA((2,)),
            pltpu.SemaphoreType.DMA((2,)),
        ],
        compiler_params=pltpu.CompilerParams(
            collective_id=0, has_side_effects=True, vmem_limit_bytes=32 * 2**20
        ),
        cost_estimate=pl.CostEstimate(flops=2 * 640 * 2048 * 4864, bytes_accessed=36 * 10**6, transcendentals=640 * 4864),
    )(hidden_rows, head_weight)
    kept = pltpu.with_memory_space_constraint(kept, pltpu.VMEM)
    scale = pltpu.with_memory_space_constraint(scale, pltpu.VMEM)
    return pl.pallas_call(
        finish,
        out_shape=jax.ShapeDtypeStruct((640, 4864), jnp.bfloat16),
        in_specs=[pl.BlockSpec(memory_space=pltpu.VMEM)] * 2,
        out_specs=pl.BlockSpec(memory_space=pl.ANY),
        scratch_shapes=[pltpu.VMEM((640, 4864), jnp.bfloat16), pltpu.SemaphoreType.DMA((20,))],
        compiler_params=pltpu.CompilerParams(vmem_limit_bytes=10 * 2**20),
        cost_estimate=pl.CostEstimate(flops=640 * 4864, bytes_accessed=19 * 10**6, transcendentals=0),
    )(kept, scale)


def solution(mesh):
    in_specs = (P(("dp", "vocab"), None), P(None, "vocab"))
    out_specs = P("dp", "vocab")
    return jax.shard_map(body, mesh=mesh, in_specs=in_specs, out_specs=out_specs, check_vma=False)
```

```python
import jax
import jax.numpy as jnp
from jax import lax
from jax.experimental import pallas as pl
from jax.experimental.pallas import tpu as pltpu
from jax.sharding import PartitionSpec as P

MESH = pl.DeviceIdType.MESH
F32 = jnp.float32
BLOCK = 40
HALF = 1024
GROUPS = (
    ((0, 0),),
    ((3, 0), (1, 0), (0, 3), (0, 1)),
    ((2, 0), (3, 3), (3, 1)),
    ((1, 3), (1, 1), (2, 3), (2, 1)),
    ((0, 2), (3, 2), (1, 2), (2, 2)),
)
ARRIVALS = tuple((da, db, half) for da in range(4) for db in range(4) for half in (0, 1) if (da, db) != (0, 0))
PEERS = tuple(sorted(
    ((da, db) for da in range(4) for db in range(4) if (da, db) != (0, 0)),
    key=lambda p: -(min(p[0], 4 - p[0]) + min(p[1], 4 - p[1])),
))


def size_of(group):
    return max(len(group) * BLOCK, 128)


def to_row(tile):
    return jnp.transpose(tile)


def to_column(row):
    return jnp.transpose(jnp.broadcast_to(row, (128, 128)))


def kernel(x_hbm, w_hbm, kept, scale, w, xb, xs, square, lane, peak_col, row_send, row_recv,
           w_sem, own_sem, send_sem, recv_sem, row_send_sem, row_recv_sem):
    core = lax.rem(lax.axis_index("dp"), 2)
    me = lax.axis_index("vocab")
    y, z = me // 4, lax.rem(me, 4)
    a, b = z + core * (y - z), y + core * (z - y)
    stride_a, stride_b = 1 + 3 * core, 4 - 3 * core

    def block(da, db):
        return lax.rem(a + da, 4) * stride_a + lax.rem(b + db, 4) * stride_b

    def rows_of(da, db):
        return pl.ds(pl.multiple_of(block(da, db) * BLOCK, 8), BLOCK)

    def load(i):
        depth = pl.ds(i % 2 * 1024, 1024)
        columns = pl.ds(0, 2304) if i < 2 else pl.ds(2304, 2560)
        return pltpu.make_async_copy(w_hbm.at[depth, columns], w.at[depth, columns], w_sem.at[i])

    own_copy = pltpu.make_async_copy(x_hbm, xb.at[me], own_sem)
    own_copy.start()
    for i in range(4):
        load(i).start(priority=1)

    barrier = pltpu.get_barrier_semaphore()
    neighbours = (block(1, 0), block(3, 0), block(0, 1), block(0, 3))
    for peer in neighbours:
        pl.semaphore_signal(barrier, inc=1, device_id={"vocab": peer}, device_id_type=MESH)
    pl.semaphore_wait(barrier, 4)

    started = []

    def part(ref, half):
        return ref.at[:, pl.ds(half * HALF, HALF)]

    def send(da, db, half, *directions):
        for ta, tb in directions:
            slot = ARRIVALS.index(((da - ta) % 4, (db - tb) % 4, half))
            ref = part(xb.at[block(da, db)], half)
            copy = pltpu.make_async_remote_copy(
                src_ref=ref,
                dst_ref=ref,
                send_sem=send_sem.at[slot],
                recv_sem=recv_sem.at[slot],
                device_id={"vocab": block(ta, tb)},
                device_id_type=MESH,
            )
            copy.start()
            started.append(copy)

    def arrive(da, db, *halves):
        for half in halves:
            slot = ARRIVALS.index((da, db, half))
            ref = part(xb.at[block(da, db)], half)
            pltpu.make_async_copy(ref, ref, recv_sem.at[slot]).wait()

    A_UP, A_DOWN, B_UP, B_DOWN = (1, 0), (3, 0), (0, 1), (0, 3)

    def multiply(group, columns):
        at = [rows_of(*g) for g in group]
        first = columns[0] == 0
        best = None if first else [lane[r, :] for r in at]
        for c in range(columns[0], columns[1], 256):
            out = jnp.dot(xs[:size_of(group), :], w[:, c:c + 256], preferred_element_type=F32)
            for i, r in enumerate(at):
                piece = out[i * BLOCK:(i + 1) * BLOCK]
                kept[r, c:c + 256] = piece
                top = jnp.maximum(piece[:, :128], piece[:, 128:])
                if best is None or len(best) <= i:
                    best = (best or []) + [top]
                else:
                    best[i] = jnp.maximum(best[i], top)
        for i, r in enumerate(at):
            lane[r, :] = best[i]

    def gather_group(group):
        pieces = [xb[block(*g)] for g in group]
        if len(group) * BLOCK < 128:
            pieces.append(jnp.zeros((128 - len(group) * BLOCK, 2048), jnp.bfloat16))
        xs[:size_of(group), :] = jnp.concatenate(pieces, axis=0)

    own_copy.wait()
    send(0, 0, 0, A_UP)
    send(0, 0, 1, A_DOWN)
    send(0, 0, 1, A_UP)
    send(0, 0, 0, A_DOWN)
    send(0, 0, 0, B_UP)
    send(0, 0, 1, B_DOWN)
    send(0, 0, 1, B_UP)
    send(0, 0, 0, B_DOWN)
    gather_group(GROUPS[0])
    load(0).wait()
    load(1).wait()
    multiply(GROUPS[0], (0, 2304))
    arrive(3, 0, 0)
    send(3, 0, 0, A_UP)
    arrive(1, 0, 1)
    send(1, 0, 1, A_DOWN)
    send(3, 0, 0, B_UP, B_DOWN)
    send(1, 0, 1, B_UP, B_DOWN)
    load(2).wait()
    load(3).wait()
    multiply(GROUPS[0], (2304, 4864))
    arrive(3, 0, 1)
    send(3, 0, 1, B_UP, B_DOWN)
    arrive(1, 0, 0)
    send(1, 0, 0, B_UP, B_DOWN)
    arrive(0, 3, 0)
    send(0, 3, 0, B_UP)
    arrive(0, 1, 1)
    send(0, 1, 1, B_DOWN)
    arrive(0, 3, 1)
    arrive(0, 1, 0)
    gather_group(GROUPS[1])
    multiply(GROUPS[1], (0, 2304))
    arrive(2, 0, 0)
    send(2, 0, 0, B_UP, B_DOWN)
    arrive(2, 0, 1)
    send(2, 0, 1, B_UP, B_DOWN)
    multiply(GROUPS[1], (2304, 4864))
    arrive(3, 3, 0)
    send(3, 3, 0, B_UP)
    arrive(3, 1, 1)
    send(3, 1, 1, B_DOWN)
    arrive(3, 3, 1)
    arrive(3, 1, 0)
    gather_group(GROUPS[2])
    multiply(GROUPS[2], (0, 2304))
    arrive(1, 3, 0)
    send(1, 3, 0, B_UP)
    arrive(1, 1, 1)
    send(1, 1, 1, B_DOWN)
    multiply(GROUPS[2], (2304, 4864))
    arrive(2, 3, 0)
    send(2, 3, 0, B_UP)
    arrive(2, 1, 1)
    send(2, 1, 1, B_DOWN)
    arrive(1, 3, 1)
    arrive(1, 1, 0)
    arrive(2, 3, 1)
    arrive(2, 1, 0)
    gather_group(GROUPS[3])
    multiply(GROUPS[3], (0, 4864))
    for last in GROUPS[4]:
        arrive(*last, 0, 1)
    gather_group(GROUPS[4])
    multiply(GROUPS[4], (0, 4864))

    def exchange(step):
        for i, peer in enumerate(PEERS):
            copy = pltpu.make_async_remote_copy(
                src_ref=row_send.at[step],
                dst_ref=row_recv.at[step, i],
                send_sem=row_send_sem.at[step],
                recv_sem=row_recv_sem.at[step],
                device_id={"vocab": block(*peer)},
                device_id_type=MESH,
            )
            copy.start()

    def exchanged(step):
        pltpu.make_async_copy(row_recv.at[step], row_recv.at[step], row_recv_sem.at[step]).wait()

    tiles = [slice(i * 128, (i + 1) * 128) for i in range(5)]
    for t in tiles:
        row_send[0, :, t] = jnp.max(to_row(lane[t, :]), axis=0, keepdims=True)
    exchange(0)
    for t in tiles:
        peak_col[t, :] = to_column(row_send[0, :, t])

    @pl.loop(0, 20)
    def _(i):
        r = pl.ds(pl.multiple_of(i * 32, 32), 32)
        top = peak_col[r, :]
        for c in range(0, 4864, 128):
            ratio = jnp.exp(kept[r, c:c + 128] - top)
            kept[r, c:c + 128] = ratio
            square[r, c:c + 128] = ratio * ratio

    exchanged(0)
    local = row_send[0]
    peak = jnp.maximum(local, jnp.max(row_recv[0], axis=0))
    shrink = jnp.exp(local - peak)
    for t in tiles:
        peak_col[t, :] = to_column(shrink[:, t] * 20.0)

    @pl.loop(0, 20)
    def _(i):
        r = pl.ds(pl.multiple_of(i * 32, 32), 32)
        factor = peak_col[r, :]
        total = jnp.zeros((32, 128), F32)
        for c in range(0, 4864, 128):
            ratio = kept[r, c:c + 128]
            value = jnp.minimum(jnp.maximum(square[r, c:c + 128] * factor - ratio, 0.0), ratio)
            kept[r, c:c + 128] = value
            total = total + value
        lane[r, :] = total

    for t in tiles:
        row_send[1, :, t] = jnp.sum(to_row(lane[t, :]), axis=0, keepdims=True) * shrink[:, t]
    exchange(1)
    exchanged(1)
    mass = row_send[1] + jnp.sum(row_recv[1], axis=0)
    final = shrink / mass
    for t in tiles:
        scale[t, :] = to_column(final[:, t])

    for copy in started:
        copy.wait_send()
    for step in range(2):
        pltpu.make_async_copy(row_recv.at[step], row_recv.at[step], row_send_sem.at[step]).wait()


def finish(kept, scale, out, stage, sem):
    copies = []
    for i in range(20):
        @pl.loop(0, 2)
        def _(j):
            r = pl.ds(pl.multiple_of(i * 32 + j * 16, 16), 16)
            factor = scale[r, :]
            for c in range(0, 4864, 128):
                stage[r, c:c + 128] = (kept[r, c:c + 128] * factor).astype(jnp.bfloat16)
        rows = pl.ds(i * 32, 32)
        copy = pltpu.make_async_copy(stage.at[rows, :], out.at[rows, :], sem.at[i])
        copy.start()
        copies.append(copy)
    for copy in copies:
        copy.wait()


def body(hidden_rows, head_weight):
    hidden_rows = pltpu.with_memory_space_constraint(hidden_rows, pltpu.HBM)
    kept, scale = pl.pallas_call(
        kernel,
        out_shape=(pltpu.VMEM((640, 4864), F32), pltpu.VMEM((640, 128), F32)),
        in_specs=[pl.BlockSpec(memory_space=pltpu.HBM)] * 2,
        out_specs=(pl.BlockSpec(memory_space=pltpu.VMEM),) * 2,
        scratch_shapes=[
            pltpu.VMEM((2048, 4864), jnp.bfloat16),
            pltpu.VMEM((16, BLOCK, 2048), jnp.bfloat16),
            pltpu.VMEM((4 * BLOCK, 2048), jnp.bfloat16),
            pltpu.VMEM((640, 4864), F32),
            pltpu.VMEM((640, 128), F32),
            pltpu.VMEM((640, 128), F32),
            pltpu.VMEM((2, 1, 640), F32),
            pltpu.VMEM((2, 15, 1, 640), F32),
            pltpu.SemaphoreType.DMA((4,)),
            pltpu.SemaphoreType.DMA,
            pltpu.SemaphoreType.DMA((30,)),
            pltpu.SemaphoreType.DMA((30,)),
            pltpu.SemaphoreType.DMA((2,)),
            pltpu.SemaphoreType.DMA((2,)),
        ],
        compiler_params=pltpu.CompilerParams(
            collective_id=0, has_side_effects=True, vmem_limit_bytes=42 * 2**20
        ),
        cost_estimate=pl.CostEstimate(flops=2 * 640 * 2048 * 4864, bytes_accessed=36 * 10**6, transcendentals=640 * 4864),
    )(hidden_rows, head_weight)
    kept = pltpu.with_memory_space_constraint(kept, pltpu.VMEM)
    scale = pltpu.with_memory_space_constraint(scale, pltpu.VMEM)
    return pl.pallas_call(
        finish,
        out_shape=jax.ShapeDtypeStruct((640, 4864), jnp.bfloat16),
        in_specs=[pl.BlockSpec(memory_space=pltpu.VMEM)] * 2,
        out_specs=pl.BlockSpec(memory_space=pl.ANY),
        scratch_shapes=[pltpu.VMEM((640, 4864), jnp.bfloat16), pltpu.SemaphoreType.DMA((20,))],
        compiler_params=pltpu.CompilerParams(vmem_limit_bytes=10 * 2**20),
        cost_estimate=pl.CostEstimate(flops=640 * 4864, bytes_accessed=19 * 10**6, transcendentals=0),
    )(kept, scale)


def solution(mesh):
    in_specs = (P(("dp", "vocab"), None), P(None, "vocab"))
    out_specs = P("dp", "vocab")
    return jax.shard_map(body, mesh=mesh, in_specs=in_specs, out_specs=out_specs, check_vma=False)
```

```python
import jax
import jax.numpy as jnp
from jax import lax
from jax.experimental import pallas as pl
from jax.experimental.pallas import tpu as pltpu
from jax.sharding import PartitionSpec as P

MESH = pl.DeviceIdType.MESH
F32 = jnp.float32
BLOCK = 40
HALF = 1024
GROUPS = (
    ((0, 0),),
    ((3, 0), (1, 0), (0, 3), (0, 1)),
    ((2, 0), (3, 3), (3, 1)),
    ((1, 3), (1, 1), (2, 3), (2, 1)),
    ((0, 2), (3, 2), (1, 2), (2, 2)),
)
ARRIVALS = tuple((da, db, half) for da in range(4) for db in range(4) for half in (0, 1) if (da, db) != (0, 0))
PEERS = tuple(sorted(
    ((da, db) for da in range(4) for db in range(4) if (da, db) != (0, 0)),
    key=lambda p: -(min(p[0], 4 - p[0]) + min(p[1], 4 - p[1])),
))


def size_of(group):
    return max(len(group) * BLOCK, 128)


def to_row(tile):
    return jnp.transpose(tile)


def to_column(row):
    return jnp.transpose(jnp.broadcast_to(row, (128, 128)))


def kernel(x_hbm, w_hbm, kept, scale, w, xb, xs, square, lane, peak_col, row_send, row_recv,
           w_sem, own_sem, send_sem, recv_sem, row_send_sem, row_recv_sem):
    core = lax.rem(lax.axis_index("dp"), 2)
    me = lax.axis_index("vocab")
    y, z = me // 4, lax.rem(me, 4)
    a, b = z + core * (y - z), y + core * (z - y)
    stride_a, stride_b = 1 + 3 * core, 4 - 3 * core

    def block(da, db):
        return lax.rem(a + da, 4) * stride_a + lax.rem(b + db, 4) * stride_b

    def rows_of(da, db):
        return pl.ds(pl.multiple_of(block(da, db) * BLOCK, 8), BLOCK)

    def load(i):
        depth = pl.ds(i % 2 * 1024, 1024)
        columns = pl.ds(0, 2304) if i < 2 else pl.ds(2304, 2560)
        return pltpu.make_async_copy(w_hbm.at[depth, columns], w.at[depth, columns], w_sem.at[i])

    own_copy = pltpu.make_async_copy(x_hbm, xb.at[me], own_sem)
    own_copy.start()
    for i in range(4):
        load(i).start(priority=1)

    barrier = pltpu.get_barrier_semaphore()
    neighbours = (block(1, 0), block(3, 0), block(0, 1), block(0, 3))
    for peer in neighbours:
        pl.semaphore_signal(barrier, inc=1, device_id={"vocab": peer}, device_id_type=MESH)
    pl.semaphore_wait(barrier, 4)

    started = []

    def part(ref, half):
        return ref.at[:, pl.ds(half * HALF, HALF)]

    def send(da, db, half, *directions):
        for ta, tb in directions:
            slot = ARRIVALS.index(((da - ta) % 4, (db - tb) % 4, half))
            ref = part(xb.at[block(da, db)], half)
            copy = pltpu.make_async_remote_copy(
                src_ref=ref,
                dst_ref=ref,
                send_sem=send_sem.at[slot],
                recv_sem=recv_sem.at[slot],
                device_id={"vocab": block(ta, tb)},
                device_id_type=MESH,
            )
            copy.start()
            started.append(copy)

    def arrive(da, db, *halves):
        for half in halves:
            slot = ARRIVALS.index((da, db, half))
            ref = part(xb.at[block(da, db)], half)
            pltpu.make_async_copy(ref, ref, recv_sem.at[slot]).wait()

    A_UP, A_DOWN, B_UP, B_DOWN = (1, 0), (3, 0), (0, 1), (0, 3)

    def multiply(group, columns):
        at = [rows_of(*g) for g in group]
        first = columns[0] == 0
        best = None if first else [lane[r, :] for r in at]
        for c in range(columns[0], columns[1], 256):
            out = jnp.dot(xs[:size_of(group), :], w[:, c:c + 256], preferred_element_type=F32)
            for i, r in enumerate(at):
                piece = out[i * BLOCK:(i + 1) * BLOCK]
                kept[r, c:c + 256] = piece
                top = jnp.maximum(piece[:, :128], piece[:, 128:])
                if best is None or len(best) <= i:
                    best = (best or []) + [top]
                else:
                    best[i] = jnp.maximum(best[i], top)
        for i, r in enumerate(at):
            lane[r, :] = best[i]

    def gather_group(group):
        pieces = [xb[block(*g)] for g in group]
        if len(group) * BLOCK < 128:
            pieces.append(jnp.zeros((128 - len(group) * BLOCK, 2048), jnp.bfloat16))
        xs[:size_of(group), :] = jnp.concatenate(pieces, axis=0)

    own_copy.wait()
    send(0, 0, 0, A_UP)
    send(0, 0, 1, A_DOWN)
    send(0, 0, 1, A_UP)
    send(0, 0, 0, A_DOWN)
    send(0, 0, 0, B_UP)
    send(0, 0, 1, B_DOWN)
    send(0, 0, 1, B_UP)
    send(0, 0, 0, B_DOWN)
    gather_group(GROUPS[0])
    load(0).wait()
    load(1).wait()
    multiply(GROUPS[0], (0, 2304))
    arrive(3, 0, 0)
    send(3, 0, 0, A_UP)
    arrive(1, 0, 1)
    send(1, 0, 1, A_DOWN)
    send(3, 0, 0, B_UP, B_DOWN)
    send(1, 0, 1, B_UP, B_DOWN)
    load(2).wait()
    load(3).wait()
    multiply(GROUPS[0], (2304, 4864))
    arrive(3, 0, 1)
    send(3, 0, 1, B_UP, B_DOWN)
    arrive(1, 0, 0)
    send(1, 0, 0, B_UP, B_DOWN)
    arrive(0, 3, 0)
    send(0, 3, 0, B_UP)
    arrive(0, 1, 1)
    send(0, 1, 1, B_DOWN)
    arrive(0, 3, 1)
    arrive(0, 1, 0)
    gather_group(GROUPS[1])
    multiply(GROUPS[1], (0, 2304))
    arrive(2, 0, 0)
    send(2, 0, 0, B_UP, B_DOWN)
    arrive(2, 0, 1)
    send(2, 0, 1, B_UP, B_DOWN)
    multiply(GROUPS[1], (2304, 4864))
    arrive(3, 3, 0)
    send(3, 3, 0, B_UP)
    arrive(3, 1, 1)
    send(3, 1, 1, B_DOWN)
    arrive(3, 3, 1)
    arrive(3, 1, 0)
    gather_group(GROUPS[2])
    multiply(GROUPS[2], (0, 2304))
    arrive(1, 3, 0)
    send(1, 3, 0, B_UP)
    arrive(1, 1, 1)
    send(1, 1, 1, B_DOWN)
    multiply(GROUPS[2], (2304, 4864))
    arrive(2, 3, 0)
    send(2, 3, 0, B_UP)
    arrive(2, 1, 1)
    send(2, 1, 1, B_DOWN)
    arrive(1, 3, 1)
    arrive(1, 1, 0)
    arrive(2, 3, 1)
    arrive(2, 1, 0)
    gather_group(GROUPS[3])
    multiply(GROUPS[3], (0, 4864))
    for last in GROUPS[4]:
        arrive(*last, 0, 1)
    gather_group(GROUPS[4])
    multiply(GROUPS[4], (0, 4864))

    def exchange(step):
        for i, peer in enumerate(PEERS):
            copy = pltpu.make_async_remote_copy(
                src_ref=row_send.at[step],
                dst_ref=row_recv.at[step, i],
                send_sem=row_send_sem.at[step],
                recv_sem=row_recv_sem.at[step],
                device_id={"vocab": block(*peer)},
                device_id_type=MESH,
            )
            copy.start()

    def exchanged(step):
        pltpu.make_async_copy(row_recv.at[step], row_recv.at[step], row_recv_sem.at[step]).wait()

    def sent(step):
        pltpu.make_async_copy(row_recv.at[step], row_recv.at[step], row_send_sem.at[step]).wait()

    tiles = [slice(i * 128, (i + 1) * 128) for i in range(5)]
    for t in tiles:
        row_send[0, :, t] = jnp.max(to_row(lane[t, :]), axis=0, keepdims=True)
    exchange(0)
    for t in tiles:
        peak_col[t, :] = to_column(row_send[0, :, t])

    @pl.loop(0, 20)
    def _(i):
        r = pl.ds(pl.multiple_of(i * 32, 32), 32)
        top = peak_col[r, :]
        for c in range(0, 4864, 128):
            ratio = jnp.exp(kept[r, c:c + 128] - top)
            kept[r, c:c + 128] = ratio
            square[r, c:c + 128] = ratio * ratio

    for copy in started:
        copy.wait_send()
    exchanged(0)
    sent(0)
    local = row_send[0]
    peak = jnp.maximum(local, jnp.max(row_recv[0], axis=0))
    shrink = jnp.exp(local - peak)
    for t in tiles:
        peak_col[t, :] = to_column(shrink[:, t] * 20.0)

    @pl.loop(0, 10)
    def _(i):
        r = pl.ds(pl.multiple_of(i * 64, 64), 64)
        factor = peak_col[r, :]
        total = jnp.zeros((64, 128), F32)
        for c in range(0, 4864, 128):
            ratio = kept[r, c:c + 128]
            value = jnp.minimum(jnp.maximum(square[r, c:c + 128] * factor - ratio, 0.0), ratio)
            kept[r, c:c + 128] = value
            total = total + value
        lane[r, :] = total

    for t in tiles:
        row_send[1, :, t] = jnp.sum(to_row(lane[t, :]), axis=0, keepdims=True) * shrink[:, t]
    exchange(1)
    exchanged(1)
    mass = row_send[1] + jnp.sum(row_recv[1], axis=0)
    scale[...] = shrink / mass

    sent(1)


def finish(kept, scale, out, column, stage, sem):
    copies = []
    for i in range(20):
        if i % 4 == 0:
            column[...] = to_column(scale[:, i * 32:i * 32 + 128])
        for j in range(0, 32, 16):
            r = slice(i * 32 + j, i * 32 + j + 16)
            factor = column[i % 4 * 32 + j:i % 4 * 32 + j + 16, :]
            for c in range(0, 4864, 128):
                stage[r, c:c + 128] = (kept[r, c:c + 128] * factor).astype(jnp.bfloat16)
        rows = pl.ds(i * 32, 32)
        copy = pltpu.make_async_copy(stage.at[rows, :], out.at[rows, :], sem.at[i])
        copy.start()
        copies.append(copy)
    for copy in copies:
        copy.wait()


def body(hidden_rows, head_weight):
    hidden_rows = pltpu.with_memory_space_constraint(hidden_rows, pltpu.HBM)
    kept, scale = pl.pallas_call(
        kernel,
        out_shape=(pltpu.VMEM((640, 4864), F32), pltpu.VMEM((1, 640), F32)),
        in_specs=[pl.BlockSpec(memory_space=pltpu.HBM)] * 2,
        out_specs=(pl.BlockSpec(memory_space=pltpu.VMEM),) * 2,
        scratch_shapes=[
            pltpu.VMEM((2048, 4864), jnp.bfloat16),
            pltpu.VMEM((16, BLOCK, 2048), jnp.bfloat16),
            pltpu.VMEM((4 * BLOCK, 2048), jnp.bfloat16),
            pltpu.VMEM((640, 4864), F32),
            pltpu.VMEM((640, 128), F32),
            pltpu.VMEM((640, 128), F32),
            pltpu.VMEM((2, 1, 640), F32),
            pltpu.VMEM((2, 15, 1, 640), F32),
            pltpu.SemaphoreType.DMA((4,)),
            pltpu.SemaphoreType.DMA,
            pltpu.SemaphoreType.DMA((30,)),
            pltpu.SemaphoreType.DMA((30,)),
            pltpu.SemaphoreType.DMA((2,)),
            pltpu.SemaphoreType.DMA((2,)),
        ],
        compiler_params=pltpu.CompilerParams(
            collective_id=0, has_side_effects=True, vmem_limit_bytes=42 * 2**20
        ),
        cost_estimate=pl.CostEstimate(flops=2 * 640 * 2048 * 4864, bytes_accessed=36 * 10**6, transcendentals=640 * 4864),
    )(hidden_rows, head_weight)
    kept = pltpu.with_memory_space_constraint(kept, pltpu.VMEM)
    scale = pltpu.with_memory_space_constraint(scale, pltpu.VMEM)
    return pl.pallas_call(
        finish,
        out_shape=jax.ShapeDtypeStruct((640, 4864), jnp.bfloat16),
        in_specs=[pl.BlockSpec(memory_space=pltpu.VMEM)] * 2,
        out_specs=pl.BlockSpec(memory_space=pl.ANY),
        scratch_shapes=[
            pltpu.VMEM((128, 128), F32),
            pltpu.VMEM((640, 4864), jnp.bfloat16),
            pltpu.SemaphoreType.DMA((20,)),
        ],
        compiler_params=pltpu.CompilerParams(vmem_limit_bytes=10 * 2**20),
        cost_estimate=pl.CostEstimate(flops=640 * 4864, bytes_accessed=19 * 10**6, transcendentals=0),
    )(kept, scale)


def solution(mesh):
    in_specs = (P(("dp", "vocab"), None), P(None, "vocab"))
    out_specs = P("dp", "vocab")
    return jax.shard_map(body, mesh=mesh, in_specs=in_specs, out_specs=out_specs, check_vma=False)
```
